32 devices in a mesh: dp: 2 (over y), seq: 16 (over z, x, core).
Axes of the slice: x: 2, y: 2, z: 4, core: 2. Of those that a mesh axis runs over, the one named last changes fastest.
Arguments:
- queries: bfloat16 [2, 2048, 2048], P('dp', 'seq'), may hold values from -6 to 6
- keys: bfloat16 [2, 2048, 2048], P('dp', 'seq'), may hold values from -6 to 6
- values: bfloat16 [2, 2048, 2048], P('dp', 'seq'), may hold values from -6 to 6
- lengths: int32 [2], P('dp'), may hold values from 512 to 2048, as said below
- norm_gain: float32 [2048], replicated, may hold values from 0.1 to 1.9
- out_weight: bfloat16 [2048, 2048], P('seq', 'dp'), may hold values from -0.125 to 0.125
Outputs:
- projected: bfloat16 [2, 2048, 2048], P('dp', 'seq')
The draws below stay inside these ranges and needn't reach their ends.
Inputs may be any that keep to these rules, and one draw needn't show every extreme that they name: `lengths`: each length is a multiple of 128; in every draw some document has the full 2048 tokens.
All inputs are finite; a program needn't handle non-finite values.
Results may differ from the reference program's by a relative error of at most 0.005.
Values may be sent and summed in bfloat16 or wider, within the bound.
A program may use at most 192 MiB of HBM per device.

```python
import jax
import jax.numpy as jnp
from jax import lax

HEADS = 16
HEAD = 128
OUTW = 2048
BLOCK = 128
HIDDEN_WIDTH = 2048
TOKENS = 2048
GROUPS = 2


def draw_lengths(key, part):
    nblocks = TOKENS // BLOCK
    lowest = max(1, nblocks // 4)
    first_key = jax.random.fold_in(key, 11)
    second_key = jax.random.fold_in(key, 23)
    counts = jax.random.randint(first_key, (GROUPS,), lowest, nblocks)
    chosen = jax.random.randint(second_key, (), 0, GROUPS)
    counts = jnp.where(jnp.arange(GROUPS) == chosen, nblocks, counts)
    return (counts * BLOCK).astype(jnp.int32)


def shard_levels(own_key, dims, shards, least, largest):
    def one(axis_at, shards_of):
        heights = jax.random.uniform(jax.random.fold_in(jax.random.fold_in(own_key, 6), axis_at), (shards_of,), jnp.float32, least / len(shards), largest / len(shards))
        return jnp.repeat(jnp.exp(heights), dims[axis_at] // shards_of).reshape((-1,) + (1,) * (len(dims) - axis_at - 1))

    gain = one(*shards[0])
    for cut in shards[1:]:
        gain = gain * one(*cut)
    return gain


def noise(rng, extent, spread, most, cuts=(), dtype=jnp.bfloat16):
    drawn = jax.random.normal(rng, extent, jnp.float32) * spread
    if len(cuts) > 0:
        drawn = shard_levels(rng, extent, cuts, -0.22, 0.18) * drawn
    return jnp.clip(drawn, min=-most, max=most).astype(dtype)


def setup_inputs(seed: int = 0) -> dict:
    streams_of = jax.random.split(jax.random.key(seed), 7)
    return {
        "queries": noise(streams_of[0], (GROUPS, TOKENS, HIDDEN_WIDTH), 1.0, 6.0, ((0, 2), (1, 16))),
        "keys": noise(streams_of[1], (GROUPS, TOKENS, HIDDEN_WIDTH), 1.0, 6.0, ((0, 2), (1, 16))),
        "values": noise(streams_of[2], (GROUPS, TOKENS, HIDDEN_WIDTH), 1.0, 6.0, ((0, 2), (1, 16))),
        "lengths": draw_lengths(jax.random.fold_in(streams_of[6], 71), 0),
        "norm_gain": jnp.clip(1.0 + 0.18 * jax.random.normal(streams_of[4], (HIDDEN_WIDTH,), jnp.float32), 0.1, 1.9),
        "out_weight": noise(streams_of[5], (HIDDEN_WIDTH, OUTW), HIDDEN_WIDTH ** -0.5, 0.125, ((0, 16), (1, 2))),
    }


def run_document(query_doc, key_doc, value_doc, length, norm_gain, out_weight):
    nblk = TOKENS // BLOCK
    shape = (nblk, BLOCK, HEADS, HEAD)
    query_blocks = query_doc.reshape(shape)
    key_blocks = key_doc.reshape(shape)
    value_blocks = value_doc.reshape(shape)
    causal = jnp.arange(BLOCK)[:, None] >= jnp.arange(BLOCK)[None, :]
    high = lax.Precision.HIGHEST

    def step(state, block):
        query_b, key_b, value_b = block
        query_f = query_b.astype(jnp.float32)
        key_f = key_b.astype(jnp.float32)
        value_f = value_b.astype(jnp.float32)
        scores = jnp.einsum('thd,shd->hts', query_f, key_f, precision=high)
        scores = jnp.where(causal[None], scores, 0.0).astype(jnp.bfloat16)
        local = jnp.einsum('hts,shd->thd', scores.astype(jnp.float32), value_f, precision=high)
        cross = jnp.einsum('thd,hde->the', query_f, state, precision=high)
        state = state + jnp.einsum('shd,she->hde', key_f, value_f, precision=high)
        return (state, local + cross)
    start = jnp.zeros((HEADS, HEAD, HEAD), jnp.float32)
    final_state, mixed = lax.scan(step, start, (query_blocks, key_blocks, value_blocks))
    mixed = mixed.reshape(TOKENS, HEADS, HEAD)
    meansq = lax.optimization_barrier(jnp.mean(mixed * mixed, axis=-1, keepdims=True))
    normed = mixed * lax.rsqrt(meansq + 1e-06) * norm_gain.reshape(HEADS, HEAD)
    valid = jnp.arange(TOKENS) < length
    normed = jnp.where(valid[:, None, None], normed, 0.0).astype(jnp.bfloat16)
    normed = normed.reshape(TOKENS, HEADS * HEAD)
    return jnp.dot(normed, out_weight, preferred_element_type=jnp.float32).astype(jnp.bfloat16)

def reference(queries, keys, values, lengths, norm_gain, out_weight):
    results = []
    for group in range(GROUPS):
        results.append(run_document(queries[group], keys[group], values[group], lengths[group], norm_gain, out_weight))
    return jnp.stack(results)
```

```python
import functools
import math

import jax
import jax.numpy as jnp
from jax import lax
from jax.experimental import pallas as pl
from jax.experimental.pallas import tpu as pltpu
from jax.sharding import PartitionSpec as P

HEAD = 128
SPLITS = 2
MESH = pl.DeviceIdType.MESH
F32 = jnp.float32
BF16 = jnp.bfloat16


def aligned(index, size):
    return pl.ds(pl.multiple_of(index * size, size), size)


def kernel(
    docs, ring,
    q_ref, k_ref, v_ref, len_ref, gain_ref, w_ref, out_ref,
    weight, state, heard, carry_in, carry_out, handed, prior, scores, normed, partial, landed,
    w_recv, wz_send, wx_send, ws_send, a_send, a_recv, b_send, b_recv, c_send, c_recv,
    n_send, n_recv, o_send, o_recv,
):
    plane = math.isqrt(ring)
    layers = ring // plane
    chips = plane // 2
    width = q_ref.shape[1]
    heads = width // HEAD
    group = width // plane
    piece = group // SPLITS
    piece_heads = piece // HEAD
    rows = width // ring
    columns = w_ref.shape[1]
    tok = q_ref.shape[0]

    doc = lax.axis_index("dp")
    me = lax.axis_index("seq")
    layer, spot = me // plane, me % plane
    chip, core = spot // 2, spot % 2
    sibling = me + 1 - 2 * core

    def remote(src, dst, send, recv, where):
        return pltpu.make_async_remote_copy(
            src_ref=src, dst_ref=dst, send_sem=send, recv_sem=recv,
            device_id=where, device_id_type=MESH,
        )

    mates = [layer * plane + (spot + i) % plane for i in range(1, plane)]
    columns_of = [((layer + i) % layers) * plane + spot for i in range(1, layers)]
    barrier = pltpu.get_barrier_semaphore()
    for other in mates + columns_of:
        pl.semaphore_signal(barrier, inc=1, device_id=(doc, other), device_id_type=MESH)
    for i in range(1, docs):
        pl.semaphore_signal(
            barrier, inc=1, device_id=((doc + i) % docs, me), device_id_type=MESH
        )
    pl.semaphore_wait(barrier, plane - 1 + layers - 1 + docs - 1)

    sent = []

    def make_state(first):
        for h in range(piece_heads):
            at = aligned(first + h, HEAD)
            state[at, :] = lax.dot_general(
                k_ref[:, at], v_ref[:, at], (((0,), (0,)), ((), ())),
                preferred_element_type=F32,
            ).astype(BF16)

    per_group = group // HEAD

    def a_copy(owner, source, j):
        return remote(
            state.at[aligned(owner * SPLITS + j, piece)],
            heard.at[source, pl.ds(j * piece, piece)],
            a_send.at[owner, j], a_recv.at[source, j],
            (doc, layer * plane + owner),
        )

    for j in range(SPLITS):
        for i in range(1, plane):
            owner = (spot + i) % plane
            make_state(owner * per_group + j * piece_heads)
            copy = a_copy(owner, spot, j)
            copy.start()
            sent.append(copy)
        make_state(spot * per_group + j * piece_heads)
        heard[spot, pl.ds(j * piece, piece), :] = state[aligned(spot * SPLITS + j, piece), :]

    def w_at(block):
        return weight.at[aligned(block, rows)]

    def w_copy(src, block, send, to):
        return remote(src, w_at(block), send, w_recv.at[block], (doc, to))

    def w_wait(block):
        w_copy(w_at(block), block, wz_send.at[0], me).wait_recv()

    def w_start(src, block, send, to):
        copy = w_copy(src, block, send, to)
        copy.start()
        sent.append(copy)

    def to_chips(src, block, slot):
        for i in range(1, chips):
            there = layer * plane + ((chip + i) % chips) * 2 + core
            w_start(src, block, wx_send.at[i, slot], there)

    for i in range(1, layers):
        there = ((layer + i) % layers) * plane + spot
        w_start(w_ref, me, wz_send.at[i], there)
    to_chips(w_ref, me, 0)
    w_start(w_ref, me, ws_send.at[0], sibling)
    weight[aligned(me, rows), :] = w_ref[...]

    rowid = lax.broadcasted_iota(jnp.int32, (tok, tok), 0)
    colid = lax.broadcasted_iota(jnp.int32, (tok, tok), 1)
    causal = rowid >= colid
    for h in range(heads):
        at = pl.ds(h * HEAD, HEAD)
        s = lax.dot_general(
            q_ref[:, at], k_ref[:, at], (((1,), (1,)), ((), ())), preferred_element_type=F32
        )
        scores[:, at] = jnp.where(causal, s, 0.0).astype(BF16)

    def b_copy(j):
        return remote(
            carry_out.at[pl.ds(j * piece, piece)], carry_in.at[pl.ds(j * piece, piece)],
            b_send.at[j], b_recv.at[j], (doc, me + plane),
        )

    def c_copy(target, owner, j):
        return remote(
            handed.at[target, pl.ds(j * piece, piece)],
            prior.at[aligned(owner * SPLITS + j, piece)],
            c_send.at[target, j], c_recv.at[owner, j],
            (doc, layer * plane + target),
        )

    for j in range(SPLITS):
        at = pl.ds(j * piece, piece)
        for i in range(1, plane):
            a_copy(spot, (spot + i) % plane, j).wait_recv()
        total = heard[0, at, :].astype(F32)
        for p in range(1, plane):
            total = total + heard[p, at, :].astype(F32)

        @pl.when(layer == 0)
        def _():
            carry_in[at, :] = jnp.zeros((piece, HEAD), BF16)

        @pl.when(layer > 0)
        def _():
            b_copy(j).wait_recv()

        before = carry_in[at, :].astype(F32)
        carry_out[at, :] = (before + total).astype(BF16)

        @pl.when(layer < layers - 1)
        def _():
            b_copy(j).start()

        for p in range(plane):
            handed[p, at, :] = before.astype(BF16)
            if p < plane - 1:
                before = before + heard[p, at, :].astype(F32)
        for i in range(1, plane):
            copy = c_copy((spot + i) % plane, spot, j)
            copy.start()
            sent.append(copy)
        prior[aligned(spot * SPLITS + j, piece), :] = handed[spot, at, :]

    for i in range(1, layers):
        block = ((layer + layers - i) % layers) * plane + spot
        w_wait(block)
        to_chips(w_at(block), block, i)
        w_start(w_at(block), block, ws_send.at[i], sibling)

    position = me * tok + lax.broadcasted_iota(jnp.int32, (tok, HEAD), 0)
    valid = position < len_ref[0]

    def n_copy(target, source, chunk):
        at = aligned(chunk, piece)
        return remote(
            normed.at[source, :, at], normed.at[source, :, at],
            n_send.at[target, chunk], n_recv.at[source, chunk], (target, me),
        )

    for i in range(plane):
        owner = (spot + plane - i) % plane
        for j in range(SPLITS):
            if i > 0:
                c_copy(spot, owner, j).wait_recv()
            for h in range(piece_heads):
                at = aligned(owner * per_group + j * piece_heads + h, HEAD)
                left = jnp.concatenate([scores[:, at], q_ref[:, at]], axis=1)
                right = jnp.concatenate([v_ref[:, at], prior[at, :]], axis=0)
                mixed = jnp.dot(left, right, preferred_element_type=F32)
                meansq = jnp.mean(mixed * mixed, axis=-1, keepdims=True)
                result = mixed * lax.rsqrt(meansq + 1e-06) * gain_ref[:, at]
                normed[doc, :, at] = jnp.where(valid, result, 0.0).astype(BF16)
            for e in range(1, docs):
                copy = n_copy((doc + e) % docs, doc, owner * SPLITS + j)
                copy.start()
                sent.append(copy)

    for i in range(1, chips):
        for zz in range(layers):
            block = (
                ((layer + layers - zz) % layers) * plane + ((chip + chips - i) % chips) * 2 + core
            )
            w_wait(block)
            w_start(w_at(block), block, ws_send.at[i * layers + zz], sibling)
    for c in range(chips):
        for zz in range(layers):
            w_wait(zz * plane + c * 2 + 1 - core)

    parts = o_send.shape[1]
    part = columns // parts

    def o_copy(target, source, j):
        at = pl.ds(j * part, part)
        return remote(
            partial.at[target, :, at], landed.at[source, :, at],
            o_send.at[target, j], o_recv.at[source, j], (target, me),
        )

    for e in range(1, docs + 1):
        other = (doc + e) % docs
        if e < docs:
            for chunk in range(plane * SPLITS):
                n_copy(doc, other, chunk).wait_recv()
        for j in range(parts):
            at = pl.ds(j * part, part)
            result = jnp.dot(
                normed[other], weight[:, at], preferred_element_type=F32
            ).astype(BF16)
            if e < docs:
                partial[other, :, at] = result
                copy = o_copy(other, doc, j)
                copy.start()
                sent.append(copy)
            else:
                landed[doc, :, at] = result
    for e in range(1, docs):
        for j in range(parts):
            o_copy(doc, (doc + e) % docs, j).wait_recv()
    for e in range(docs):
        out_ref[:, pl.ds(e * columns, columns)] = landed[e]

    @pl.when(layer < layers - 1)
    def _():
        for j in range(SPLITS):
            b_copy(j).wait_send()

    for copy in sent:
        copy.wait_send()


def body(docs, ring, queries, keys, values, lengths, norm_gain, out_weight):
    _, tok, width = queries.shape
    columns = out_weight.shape[1]
    plane = math.isqrt(ring)
    layers = ring // plane
    chips = plane // 2
    group = width // plane
    parts = max(1, columns // 512)
    vmem = pl.BlockSpec(memory_space=pltpu.VMEM)
    dma = pltpu.SemaphoreType.DMA
    out = pl.pallas_call(
        functools.partial(kernel, docs, ring),
        out_shape=jax.ShapeDtypeStruct((tok, width), BF16),
        in_specs=[vmem, vmem, vmem, pl.BlockSpec(memory_space=pltpu.SMEM), vmem, vmem],
        out_specs=vmem,
        scratch_shapes=[
            pltpu.VMEM((width, columns), BF16),
            pltpu.VMEM((width, HEAD), BF16),
            pltpu.VMEM((plane, group, HEAD), BF16),
            pltpu.VMEM((group, HEAD), BF16),
            pltpu.VMEM((group, HEAD), BF16),
            pltpu.VMEM((plane, group, HEAD), BF16),
            pltpu.VMEM((width, HEAD), BF16),
            pltpu.VMEM((tok, width), BF16),
            pltpu.VMEM((docs, tok, width), BF16),
            pltpu.VMEM((docs, tok, columns), BF16),
            pltpu.VMEM((docs, tok, columns), BF16),
            dma((ring,)),
            dma((layers,)),
            dma((chips, layers)),
            dma((chips * layers,)),
            dma((plane, SPLITS)),
            dma((plane, SPLITS)),
            dma((SPLITS,)),
            dma((SPLITS,)),
            dma((plane, SPLITS)),
            dma((plane, SPLITS)),
            dma((docs, plane * SPLITS)),
            dma((docs, plane * SPLITS)),
            dma((docs, parts)),
            dma((docs, parts)),
        ],
        compiler_params=pltpu.CompilerParams(
            collective_id=0, has_side_effects=True, vmem_limit_bytes=48 * 1024 * 1024
        ),
        cost_estimate=pl.CostEstimate(
            flops=2 * tok * width * (width + 4 * HEAD),
            bytes_accessed=8 * tok * width,
            transcendentals=tok * (width // HEAD),
        ),
    )(
        queries.reshape(tok, width),
        keys.reshape(tok, width),
        values.reshape(tok, width),
        lengths,
        norm_gain.reshape(1, width),
        out_weight,
    )
    return out[None]


def solution(mesh):
    in_specs = (
        P("dp", "seq", None),
        P("dp", "seq", None),
        P("dp", "seq", None),
        P("dp"),
        P(),
        P("seq", "dp"),
    )
    out_specs = P("dp", "seq", None)
    run = functools.partial(body, mesh.shape["dp"], mesh.shape["seq"])
    return jax.shard_map(run, mesh=mesh, in_specs=in_specs, out_specs=out_specs, check_vma=False)
```

```python
import functools
import math

import jax
import jax.numpy as jnp
from jax import lax
from jax.experimental import pallas as pl
from jax.experimental.pallas import tpu as pltpu
from jax.sharding import PartitionSpec as P

HEAD = 128
SPLITS = 2
MESH = pl.DeviceIdType.MESH
F32 = jnp.float32
BF16 = jnp.bfloat16


def aligned(index, size):
    return pl.ds(pl.multiple_of(index * size, size), size)


def kernel(
    docs, ring,
    q_ref, k_ref, v_ref, len_ref, gain_ref, w_ref, out_ref,
    weight, state, heard, carry_in, carry_out, handed, prior, scores, normed, partial, landed,
    w_recv, wz_send, wx_send, ws_send, a_send, a_recv, b_send, b_recv, c_send, c_recv,
    n_send, n_recv, o_send, o_recv,
):
    plane = math.isqrt(ring)
    layers = ring // plane
    chips = plane // 2
    width = q_ref.shape[1]
    heads = width // HEAD
    group = width // plane
    piece = group // SPLITS
    piece_heads = piece // HEAD
    rows = width // ring
    columns = w_ref.shape[1]
    tok = q_ref.shape[0]

    doc = lax.axis_index("dp")
    me = lax.axis_index("seq")
    layer, spot = me // plane, me % plane
    chip, core = spot // 2, spot % 2
    sibling = me + 1 - 2 * core

    def remote(src, dst, send, recv, where):
        return pltpu.make_async_remote_copy(
            src_ref=src, dst_ref=dst, send_sem=send, recv_sem=recv,
            device_id=where, device_id_type=MESH,
        )

    mates = [layer * plane + (spot + i) % plane for i in range(1, plane)]
    columns_of = [((layer + i) % layers) * plane + spot for i in range(1, layers)]
    barrier = pltpu.get_barrier_semaphore()
    for other in mates + columns_of:
        pl.semaphore_signal(barrier, inc=1, device_id=(doc, other), device_id_type=MESH)
    for i in range(1, docs):
        pl.semaphore_signal(
            barrier, inc=1, device_id=((doc + i) % docs, me), device_id_type=MESH
        )
    pl.semaphore_wait(barrier, plane - 1 + layers - 1 + docs - 1)

    sent = []
    maybe = []

    def w_at(high, across, side=None):
        block = high * plane + across * 2 + (core if side is None else side)
        return weight.at[aligned(block, rows)], w_recv.at[block]

    def w_copy(src, high, across, send, to):
        dst, recv = w_at(high, across)
        return remote(dst if src is None else src, dst, send, recv, (doc, to))

    def w_start(src, high, across, send, to, cond=None):
        if cond is None:
            copy = w_copy(src, high, across, send, to)
            copy.start()
            sent.append(copy)
        else:
            @pl.when(cond)
            def _():
                w_copy(src, high, across, send, to).start()

            maybe.append((cond, lambda: w_copy(src, high, across, send, to)))

    def w_wait(high, across, side=None):
        dst, recv = w_at(high, across, side)
        remote(dst, dst, wz_send.at[0, 0], recv, (doc, me)).wait_recv()

    def chip_at(i):
        return layer * plane + ((chip + i) % chips) * 2 + core

    def up(src, t):
        cond = (layer < layers - 1) & (layer >= t)
        w_start(src, jnp.maximum(layer - t, 0), chip, wz_send.at[0, t], me + plane, cond)

    def down(src, t):
        cond = (layer > 0) & (layer + t < layers)
        w_start(src, jnp.minimum(layer + t, layers - 1), chip, wz_send.at[1, t], me - plane, cond)

    def onward(high, cond):
        for i in range(1, chips):
            w_start(None, high, chip, wx_send.at[i, high], chip_at(i), cond)
        w_start(None, high, chip, ws_send.at[0, high], sibling, cond)

    def hop(t):
        below, above = layer - t, layer + t

        @pl.when(below >= 0)
        def _():
            w_wait(below, chip)

        if t < layers - 1:
            up(None, t)
        onward(jnp.maximum(below, 0), below >= 0)

        @pl.when(above < layers)
        def _():
            w_wait(above, chip)

        if t < layers - 1:
            down(None, t)
        onward(jnp.minimum(above, layers - 1), above < layers)

    def across(t):
        for i in range(1, chips):
            other = (chip + chips - i) % chips
            for sign in (-1, 1) if t else (1,):
                high = layer + sign * t
                cond = (high >= 0) & (high < layers)
                high = jnp.clip(high, 0, layers - 1)

                @pl.when(cond)
                def _():
                    w_wait(high, other)

                w_start(None, high, other, ws_send.at[i, high], sibling, cond)

    up(w_ref, 0)
    down(w_ref, 0)

    def make_state(first):
        for h in range(piece_heads):
            at = aligned(first + h, HEAD)
            state[at, :] = lax.dot_general(
                k_ref[:, at], v_ref[:, at], (((0,), (0,)), ((), ())),
                preferred_element_type=F32,
            ).astype(BF16)

    per_group = group // HEAD

    def a_copy(owner, source, j):
        return remote(
            state.at[aligned(owner * SPLITS + j, piece)],
            heard.at[source, pl.ds(j * piece, piece)],
            a_send.at[owner, j], a_recv.at[source, j],
            (doc, layer * plane + owner),
        )

    for j in range(SPLITS):
        for i in range(1, plane):
            owner = (spot + i) % plane
            make_state(owner * per_group + j * piece_heads)
            copy = a_copy(owner, spot, j)
            copy.start()
            sent.append(copy)
        make_state(spot * per_group + j * piece_heads)
        heard[spot, pl.ds(j * piece, piece), :] = state[aligned(spot * SPLITS + j, piece), :]

    for i in range(1, chips):
        w_start(w_ref, layer, chip, wx_send.at[i, layer], chip_at(i))
    w_start(w_ref, layer, chip, ws_send.at[0, layer], sibling)
    weight[aligned(me, rows), :] = w_ref[...]

    rowid = lax.broadcasted_iota(jnp.int32, (tok, tok), 0)
    colid = lax.broadcasted_iota(jnp.int32, (tok, tok), 1)
    causal = rowid >= colid
    for h in range(heads):
        at = pl.ds(h * HEAD, HEAD)
        s = lax.dot_general(
            q_ref[:, at], k_ref[:, at], (((1,), (1,)), ((), ())), preferred_element_type=F32
        )
        scores[:, at] = jnp.where(causal, s, 0.0).astype(BF16)

    hop(1)
    def b_copy(j):
        return remote(
            carry_out.at[pl.ds(j * piece, piece)], carry_in.at[pl.ds(j * piece, piece)],
            b_send.at[j], b_recv.at[j], (doc, me + plane),
        )

    def c_copy(target, owner, j):
        return remote(
            handed.at[target, pl.ds(j * piece, piece)],
            prior.at[aligned(owner * SPLITS + j, piece)],
            c_send.at[target, j], c_recv.at[owner, j],
            (doc, layer * plane + target),
        )

    for j in range(SPLITS):
        at = pl.ds(j * piece, piece)
        for i in range(1, plane):
            a_copy(spot, (spot + i) % plane, j).wait_recv()
        total = heard[0, at, :].astype(F32)
        for p in range(1, plane):
            total = total + heard[p, at, :].astype(F32)

        @pl.when(layer == 0)
        def _():
            carry_in[at, :] = jnp.zeros((piece, HEAD), BF16)

        @pl.when(layer > 0)
        def _():
            b_copy(j).wait_recv()

        before = carry_in[at, :].astype(F32)
        carry_out[at, :] = (before + total).astype(BF16)

        @pl.when(layer < layers - 1)
        def _():
            b_copy(j).start()

        for p in range(plane):
            handed[p, at, :] = before.astype(BF16)
            if p < plane - 1:
                before = before + heard[p, at, :].astype(F32)
        for i in range(1, plane):
            copy = c_copy((spot + i) % plane, spot, j)
            copy.start()
            sent.append(copy)
        prior[aligned(spot * SPLITS + j, piece), :] = handed[spot, at, :]

    for t in range(2, layers - 1):
        hop(t)
    hop(layers - 1)
    position = me * tok + lax.broadcasted_iota(jnp.int32, (tok, HEAD), 0)
    valid = position < len_ref[0]

    def n_copy(target, source, chunk):
        at = aligned(chunk, piece)
        return remote(
            normed.at[source, :, at], normed.at[source, :, at],
            n_send.at[target, chunk], n_recv.at[source, chunk], (target, me),
        )

    for j in range(SPLITS):
        for i in range(plane):
            owner = (spot + plane - i) % plane
            if i > 0:
                c_copy(spot, owner, j).wait_recv()
            for h in range(piece_heads):
                at = aligned(owner * per_group + j * piece_heads + h, HEAD)
                left = jnp.concatenate([scores[:, at], q_ref[:, at]], axis=1)
                right = jnp.concatenate([v_ref[:, at], prior[at, :]], axis=0)
                mixed = jnp.dot(left, right, preferred_element_type=F32)
                meansq = jnp.mean(mixed * mixed, axis=-1, keepdims=True)
                result = mixed * lax.rsqrt(meansq + 1e-06) * gain_ref[:, at]
                normed[doc, :, at] = jnp.where(valid, result, 0.0).astype(BF16)
            for e in range(1, docs):
                copy = n_copy((doc + e) % docs, doc, owner * SPLITS + j)
                copy.start()
                sent.append(copy)

    for t in range(layers):
        across(t)
    for c in range(chips):
        for zz in range(layers):
            w_wait(zz, c, 1 - core)

    parts = o_send.shape[1]
    part = columns // parts

    def o_copy(target, source, j):
        at = pl.ds(j * part, part)
        return remote(
            partial.at[target, :, at], landed.at[source, :, at],
            o_send.at[target, j], o_recv.at[source, j], (target, me),
        )

    for e in range(1, docs + 1):
        other = (doc + e) % docs
        if e < docs:
            for chunk in range(plane * SPLITS):
                n_copy(doc, other, chunk).wait_recv()
        for j in range(parts):
            at = pl.ds(j * part, part)
            result = jnp.dot(
                normed[other], weight[:, at], preferred_element_type=F32
            ).astype(BF16)
            if e < docs:
                partial[other, :, at] = result
                copy = o_copy(other, doc, j)
                copy.start()
                sent.append(copy)
            else:
                landed[doc, :, at] = result
    for e in range(1, docs):
        for j in range(parts):
            o_copy(doc, (doc + e) % docs, j).wait_recv()
    for e in range(docs):
        out_ref[:, pl.ds(e * columns, columns)] = landed[e]

    @pl.when(layer < layers - 1)
    def _():
        for j in range(SPLITS):
            b_copy(j).wait_send()

    for copy in sent:
        copy.wait_send()
    for cond, again in maybe:

        @pl.when(cond)
        def _():
            again().wait_send()


def body(docs, ring, queries, keys, values, lengths, norm_gain, out_weight):
    _, tok, width = queries.shape
    columns = out_weight.shape[1]
    plane = math.isqrt(ring)
    layers = ring // plane
    chips = plane // 2
    group = width // plane
    parts = max(1, columns // 512)
    vmem = pl.BlockSpec(memory_space=pltpu.VMEM)
    dma = pltpu.SemaphoreType.DMA
    out = pl.pallas_call(
        functools.partial(kernel, docs, ring),
        out_shape=jax.ShapeDtypeStruct((tok, width), BF16),
        in_specs=[vmem, vmem, vmem, pl.BlockSpec(memory_space=pltpu.SMEM), vmem, vmem],
        out_specs=vmem,
        scratch_shapes=[
            pltpu.VMEM((width, columns), BF16),
            pltpu.VMEM((width, HEAD), BF16),
            pltpu.VMEM((plane, group, HEAD), BF16),
            pltpu.VMEM((group, HEAD), BF16),
            pltpu.VMEM((group, HEAD), BF16),
            pltpu.VMEM((plane, group, HEAD), BF16),
            pltpu.VMEM((width, HEAD), BF16),
            pltpu.VMEM((tok, width), BF16),
            pltpu.VMEM((docs, tok, width), BF16),
            pltpu.VMEM((docs, tok, columns), BF16),
            pltpu.VMEM((docs, tok, columns), BF16),
            dma((ring,)),
            dma((2, layers)),
            dma((chips, layers)),
            dma((chips, layers)),
            dma((plane, SPLITS)),
            dma((plane, SPLITS)),
            dma((SPLITS,)),
            dma((SPLITS,)),
            dma((plane, SPLITS)),
            dma((plane, SPLITS)),
            dma((docs, plane * SPLITS)),
            dma((docs, plane * SPLITS)),
            dma((docs, parts)),
            dma((docs, parts)),
        ],
        compiler_params=pltpu.CompilerParams(
            collective_id=0, has_side_effects=True, vmem_limit_bytes=48 * 1024 * 1024
        ),
        cost_estimate=pl.CostEstimate(
            flops=2 * tok * width * (width + 4 * HEAD),
            bytes_accessed=8 * tok * width,
            transcendentals=tok * (width // HEAD),
        ),
    )(
        queries.reshape(tok, width),
        keys.reshape(tok, width),
        values.reshape(tok, width),
        lengths,
        norm_gain.reshape(1, width),
        out_weight,
    )
    return out[None]


def solution(mesh):
    in_specs = (
        P("dp", "seq", None),
        P("dp", "seq", None),
        P("dp", "seq", None),
        P("dp"),
        P(),
        P("seq", "dp"),
    )
    out_specs = P("dp", "seq", None)
    run = functools.partial(body, mesh.shape["dp"], mesh.shape["seq"])
    return jax.shard_map(run, mesh=mesh, in_specs=in_specs, out_specs=out_specs, check_vma=False)
```

```python
import functools
import math

import jax
import jax.numpy as jnp
from jax import lax
from jax.experimental import pallas as pl
from jax.experimental.pallas import tpu as pltpu
from jax.sharding import PartitionSpec as P

HEAD = 128
MOST = 2
LAG = 2
FIRST = 6
PLAN = (0, 0, 2, 3, 5)
MESH = pl.DeviceIdType.MESH
F32 = jnp.float32
BF16 = jnp.bfloat16


def aligned(index, size):
    return pl.ds(pl.multiple_of(index * size, size), size)


def splits_of(group):
    return min(MOST, group // HEAD)


def split_of(columns):
    return columns * FIRST // 8 // HEAD * HEAD


def kernel(
    docs, ring,
    q_ref, k_ref, v_ref, len_ref, gain_ref, w_ref, out_ref,
    weight, state, heard, carry_in, carry_out, handed, prior, scores, normed, partial, landed,
    w_recv, wz_send, wx_send, ws_send, a_send, a_recv, b_send, b_recv, c_send, c_recv,
    n_send, n_recv, o_send, o_recv,
):
    plane = math.isqrt(ring)
    layers = ring // plane
    chips = plane // 2
    width = q_ref.shape[1]
    heads = width // HEAD
    group = width // plane
    splits = splits_of(group)
    piece = group // splits
    piece_heads = piece // HEAD
    rows = width // ring
    columns = w_ref.shape[1]
    tok = q_ref.shape[0]

    doc = lax.axis_index("dp")
    me = lax.axis_index("seq")
    layer, spot = me // plane, me % plane
    chip, core = spot // 2, spot % 2
    sibling = me + 1 - 2 * core

    def remote(src, dst, send, recv, where):
        return pltpu.make_async_remote_copy(
            src_ref=src, dst_ref=dst, send_sem=send, recv_sem=recv,
            device_id=where, device_id_type=MESH,
        )

    mates = [layer * plane + (spot + i) % plane for i in range(1, plane)]
    columns_of = [((layer + i) % layers) * plane + spot for i in range(1, layers)]
    barrier = pltpu.get_barrier_semaphore()
    for other in mates + columns_of:
        pl.semaphore_signal(barrier, inc=1, device_id=(doc, other), device_id_type=MESH)
    for i in range(1, docs):
        pl.semaphore_signal(
            barrier, inc=1, device_id=((doc + i) % docs, me), device_id_type=MESH
        )
    pl.semaphore_wait(barrier, plane - 1 + layers - 1 + docs - 1)

    sent = []
    maybe = []

    split = split_of(columns)
    cuts = (pl.ds(0, split), pl.ds(split, columns - split))

    def w_at(part, high, across, side=None):
        block = high * plane + across * 2 + (core if side is None else side)
        return weight.at[aligned(block, rows), cuts[part]], w_recv.at[part, block]

    def w_start(part, high, across, send, to, cond=None):
        def make():
            dst, recv = w_at(part, high, across)
            return remote(dst, dst, send, recv, (doc, to))

        if cond is None:
            copy = make()
            copy.start()
            sent.append(copy)
        else:
            @pl.when(cond)
            def _():
                make().start()

            maybe.append((cond, make))

    def w_wait(part, high, across, side=None):
        dst, recv = w_at(part, high, across, side)
        remote(dst, dst, wz_send.at[0, 0, 0], recv, (doc, me)).wait_recv()

    def chip_at(i):
        return layer * plane + ((chip + i) % chips) * 2 + core

    def rise(part, t, i):
        if t < layers - 1:
            cond = (layer < layers - 1) & (layer >= t)
            high = jnp.maximum(layer - t, 0)
            send = wz_send.at[0, t, part + i]
            w_start(part, high, (chip + i) % chips, send, me + plane, cond)

    def sink(part, t, i):
        if t < layers - 1:
            cond = (layer > 0) & (layer + t < layers)
            high = jnp.minimum(layer + t, layers - 1)
            send = wz_send.at[1, t, part + i]
            w_start(part, high, (chip + i) % chips, send, me - plane, cond)

    def to_chips(part, high, cond):
        for i in range(1, chips):
            w_start(part, high, chip, wx_send.at[part, i, high], chip_at(i), cond)

    def to_core(part, high, i, cond):
        across = (chip + i) % chips
        w_start(part, high, across, ws_send.at[part, i, high], sibling, cond)

    def take(part, high, across, cond):
        @pl.when(cond)
        def _():
            w_wait(part, high, across)

    def hop(t):
        below, above = layer - t, layer + t
        ways = (
            (jnp.maximum(below, 0), below >= 0, rise),
            (jnp.minimum(above, layers - 1), above < layers, sink),
        )
        for high, cond, pass_on in ways:
            take(0, high, chip, cond)
            pass_on(0, t, 0)
            to_chips(0, high, cond)
            to_core(0, high, 0, cond)
        for i in range(chips):
            for high, cond, pass_on in ways:
                take(1, high, (chip + i) % chips, cond)
                pass_on(1, t, i)
                to_core(1, high, i, cond)

    def beside():
        for i in range(1, chips):
            w_wait(1, layer, (chip + i) % chips)
            rise(1, 0, i)
            sink(1, 0, i)
            to_core(1, layer, i, None)

    def across(t):
        for i in range(1, chips):
            for sign in (-1, 1) if t else (1,):
                high = layer + sign * t
                cond = (high >= 0) & (high < layers)
                high = jnp.clip(high, 0, layers - 1)
                take(0, high, (chip + i) % chips, cond)
                to_core(0, high, i, cond)

    def stage(at):
        for step in range(2 * layers):
            if min(PLAN[min(step, len(PLAN) - 1)], splits + LAG + 1) == at:
                if step == 0:
                    beside()
                elif step < layers:
                    hop(step)
                else:
                    across(step - layers)

    weight[aligned(me, rows), :] = w_ref[...]
    to_chips(1, layer, None)
    for part in range(2):
        rise(part, 0, 0)
        sink(part, 0, 0)

    def make_state(first):
        for h in range(piece_heads):
            at = aligned(first + h, HEAD)
            state[at, :] = lax.dot_general(
                k_ref[:, at], v_ref[:, at], (((0,), (0,)), ((), ())),
                preferred_element_type=F32,
            ).astype(BF16)

    per_group = group // HEAD

    def a_copy(owner, source, j):
        return remote(
            state.at[aligned(owner * splits + j, piece)],
            heard.at[source, pl.ds(j * piece, piece)],
            a_send.at[owner, j], a_recv.at[source, j],
            (doc, layer * plane + owner),
        )

    for j in range(splits):
        for i in range(1, plane):
            owner = (spot + i) % plane
            make_state(owner * per_group + j * piece_heads)
            copy = a_copy(owner, spot, j)
            copy.start()
            sent.append(copy)
        make_state(spot * per_group + j * piece_heads)
        heard[spot, pl.ds(j * piece, piece), :] = state[aligned(spot * splits + j, piece), :]

    to_chips(0, layer, None)
    for part in range(2):
        to_core(part, layer, 0, None)

    rowid = lax.broadcasted_iota(jnp.int32, (tok, tok), 0)
    colid = lax.broadcasted_iota(jnp.int32, (tok, tok), 1)
    causal = rowid >= colid
    for h in range(heads):
        at = pl.ds(h * HEAD, HEAD)
        s = lax.dot_general(
            q_ref[:, at], k_ref[:, at], (((1,), (1,)), ((), ())), preferred_element_type=F32
        )
        scores[:, at] = jnp.where(causal, s, 0.0).astype(BF16)

    stage(0)
    def b_copy(j):
        return remote(
            carry_out.at[pl.ds(j * piece, piece)], carry_in.at[pl.ds(j * piece, piece)],
            b_send.at[j], b_recv.at[j], (doc, me + plane),
        )

    def c_copy(target, owner, j):
        return remote(
            handed.at[target, pl.ds(j * piece, piece)],
            prior.at[aligned(owner * splits + j, piece)],
            c_send.at[target, j], c_recv.at[owner, j],
            (doc, layer * plane + target),
        )

    def carry(j):
        at = pl.ds(j * piece, piece)
        for i in range(1, plane):
            a_copy(spot, (spot + i) % plane, j).wait_recv()
        total = heard[0, at, :].astype(F32)
        for p in range(1, plane):
            total = total + heard[p, at, :].astype(F32)

        @pl.when(layer == 0)
        def _():
            carry_in[at, :] = jnp.zeros((piece, HEAD), BF16)

        @pl.when(layer > 0)
        def _():
            b_copy(j).wait_recv()

        before = carry_in[at, :].astype(F32)
        carry_out[at, :] = (before + total).astype(BF16)

        @pl.when(layer < layers - 1)
        def _():
            b_copy(j).start()

        for p in range(plane):
            handed[p, at, :] = before.astype(BF16)
            if p < plane - 1:
                before = before + heard[p, at, :].astype(F32)
        for i in range(1, plane):
            copy = c_copy((spot + i) % plane, spot, j)
            copy.start()
            sent.append(copy)
        prior[aligned(spot * splits + j, piece), :] = handed[spot, at, :]

    position = me * tok + lax.broadcasted_iota(jnp.int32, (tok, HEAD), 0)
    valid = position < len_ref[0]

    def n_copy(target, source, chunk):
        at = aligned(chunk, piece)
        return remote(
            normed.at[source, :, at], normed.at[source, :, at],
            n_send.at[target, chunk], n_recv.at[source, chunk], (target, me),
        )

    def finish(j):
        for i in range(plane):
            owner = (spot + plane - i) % plane
            if i > 0:
                c_copy(spot, owner, j).wait_recv()
            for h in range(piece_heads):
                at = aligned(owner * per_group + j * piece_heads + h, HEAD)
                left = jnp.concatenate([scores[:, at], q_ref[:, at]], axis=1)
                right = jnp.concatenate([v_ref[:, at], prior[at, :]], axis=0)
                mixed = jnp.dot(left, right, preferred_element_type=F32)
                meansq = jnp.mean(mixed * mixed, axis=-1, keepdims=True)
                result = mixed * lax.rsqrt(meansq + 1e-06) * gain_ref[:, at]
                normed[doc, :, at] = jnp.where(valid, result, 0.0).astype(BF16)
            for e in range(1, docs):
                copy = n_copy((doc + e) % docs, doc, owner * splits + j)
                copy.start()
                sent.append(copy)

    for step in range(splits + LAG):
        if step < splits:
            carry(step)
        if step >= LAG:
            finish(step - LAG)
        stage(step + 1)


    stage(splits + LAG + 1)
    for c in range(chips):
        for zz in range(layers):
            for part in range(2):
                w_wait(part, zz, c, 1 - core)

    parts = o_send.shape[1]
    part = columns // parts

    def o_copy(target, source, j):
        at = pl.ds(j * part, part)
        return remote(
            partial.at[target, :, at], landed.at[source, :, at],
            o_send.at[target, j], o_recv.at[source, j], (target, me),
        )

    for e in range(1, docs + 1):
        other = (doc + e) % docs
        if e < docs:
            for chunk in range(plane * splits):
                n_copy(doc, other, chunk).wait_recv()
        for j in range(parts):
            at = pl.ds(j * part, part)
            result = jnp.dot(
                normed[other], weight[:, at], preferred_element_type=F32
            ).astype(BF16)
            if e < docs:
                partial[other, :, at] = result
                copy = o_copy(other, doc, j)
                copy.start()
                sent.append(copy)
            else:
                landed[doc, :, at] = result
    for e in range(1, docs):
        for j in range(parts):
            o_copy(doc, (doc + e) % docs, j).wait_recv()
    for e in range(docs):
        out_ref[:, pl.ds(e * columns, columns)] = landed[e]

    @pl.when(layer < layers - 1)
    def _():
        for j in range(splits):
            b_copy(j).wait_send()

    for copy in sent:
        copy.wait_send()
    for cond, again in maybe:

        @pl.when(cond)
        def _():
            again().wait_send()


def body(docs, ring, queries, keys, values, lengths, norm_gain, out_weight):
    _, tok, width = queries.shape
    columns = out_weight.shape[1]
    plane = math.isqrt(ring)
    layers = ring // plane
    chips = plane // 2
    group = width // plane
    splits = splits_of(group)
    parts = max(1, columns // 512)
    vmem = pl.BlockSpec(memory_space=pltpu.VMEM)
    dma = pltpu.SemaphoreType.DMA
    out = pl.pallas_call(
        functools.partial(kernel, docs, ring),
        out_shape=jax.ShapeDtypeStruct((tok, width), BF16),
        in_specs=[vmem, vmem, vmem, pl.BlockSpec(memory_space=pltpu.SMEM), vmem, vmem],
        out_specs=vmem,
        scratch_shapes=[
            pltpu.VMEM((width, columns), BF16),
            pltpu.VMEM((width, HEAD), BF16),
            pltpu.VMEM((plane, group, HEAD), BF16),
            pltpu.VMEM((group, HEAD), BF16),
            pltpu.VMEM((group, HEAD), BF16),
            pltpu.VMEM((plane, group, HEAD), BF16),
            pltpu.VMEM((width, HEAD), BF16),
            pltpu.VMEM((tok, width), BF16),
            pltpu.VMEM((docs, tok, width), BF16),
            pltpu.VMEM((docs, tok, columns), BF16),
            pltpu.VMEM((docs, tok, columns), BF16),
            dma((2, ring)),
            dma((2, layers, 1 + chips)),
            dma((2, chips, layers)),
            dma((2, chips, layers)),
            dma((plane, splits)),
            dma((plane, splits)),
            dma((splits,)),
            dma((splits,)),
            dma((plane, splits)),
            dma((plane, splits)),
            dma((docs, plane * splits)),
            dma((docs, plane * splits)),
            dma((docs, parts)),
            dma((docs, parts)),
        ],
        compiler_params=pltpu.CompilerParams(
            collective_id=0, has_side_effects=True, vmem_limit_bytes=48 * 1024 * 1024
        ),
        cost_estimate=pl.CostEstimate(
            flops=2 * tok * width * (width + 4 * HEAD),
            bytes_accessed=8 * tok * width,
            transcendentals=tok * (width // HEAD),
        ),
    )(
        queries.reshape(tok, width),
        keys.reshape(tok, width),
        values.reshape(tok, width),
        lengths,
        norm_gain.reshape(1, width),
        out_weight,
    )
    return out[None]


def solution(mesh):
    in_specs = (
        P("dp", "seq", None),
        P("dp", "seq", None),
        P("dp", "seq", None),
        P("dp"),
        P(),
        P("seq", "dp"),
    )
    out_specs = P("dp", "seq", None)
    run = functools.partial(body, mesh.shape["dp"], mesh.shape["seq"])
    return jax.shard_map(run, mesh=mesh, in_specs=in_specs, out_specs=out_specs, check_vma=False)
```
